32 devices in a mesh: row: 4 (over y, x), col: 8 (over z, core).
Axes of the slice: x: 2, y: 2, z: 4, core: 2. Of those that a mesh axis runs over, the one named last changes fastest.
Arguments:
- returns: bfloat16 [8192, 256], P(('col', 'row')), may hold values from -6 to 6
- start_day: int32 [8192], P(('col', 'row')), may hold values from 0 to 127
- shrink_code: int32 [1], replicated, may hold values from 64 to 191
- weights: bfloat16 [8192, 512], P(('col', 'row')), may hold values from -1.5 to 1.5
Outputs:
- exposures: float32 [8192, 512], P(('col', 'row'))
The draws below stay inside these ranges and needn't reach their ends.
All inputs are finite; a program needn't handle non-finite values.
Results may differ from the reference program's by a relative error of at most 0.0041.
Values may be sent and summed in bfloat16 or wider, within the bound.
No kernel may reach another device: no remote copies, remote signals or barrier semaphores. Data moves between devices by JAX's collectives and lax.ppermute only.
A program may use at most 128 MiB of HBM per device.

```python
import math
import jax
import jax.numpy as jnp
from jax import lax

TDAY = 256
PORT = 512
DENOM = 256
NASSET = 8192


def set_ends(entries, own_key, low, high):
    longest = entries.shape.index(max(entries.shape))
    spots = []
    for shift in (0, 1):
        where = [jax.random.randint(jax.random.fold_in(own_key, axis), (), 0, length) for axis, length in enumerate(entries.shape)]
        where[longest] = (where[longest] + shift) % entries.shape[longest]
        spots.append(tuple(where))
    return entries.at[spots[0]].set(low).at[spots[1]].set(high)


def shard_levels(key, shape, pieces, smallest, high):
    level = 1.0
    for position, shards_of in pieces:
        heights = jax.random.uniform(jax.random.fold_in(jax.random.fold_in(key, 6), position), (shards_of,), jnp.float32, smallest / len(pieces), high / len(pieces))
        level = level * jnp.repeat(jnp.exp(heights), shape[position] // shards_of).reshape((-1,) + (1,) * (len(shape) - 1 - position))
    return level


def scatter_about(stream_key, shape, scale, limit, cuts=(), kind=jnp.bfloat16):
    gain = shard_levels(stream_key, shape, cuts, -0.22, 0.18) if cuts else 1.0
    result = jax.random.normal(stream_key, shape, jnp.float32) * scale * gain
    return jnp.minimum(jnp.maximum(result, -limit), limit).astype(kind)


def setup_inputs(seed: int = 0) -> dict:
    key_list = jax.random.split(jax.random.key(seed), 5)
    return {
        "returns": scatter_about(key_list[0], (NASSET, TDAY), 1.0, 6.0, ((0, 32),)),
        "start_day": set_ends(jax.random.randint(key_list[1], (NASSET,), 0, TDAY // 2), jax.random.fold_in(key_list[1], 1), 0, (TDAY // 2) - 1).astype(jnp.int32),
        "shrink_code": jax.random.randint(key_list[2], (1,), 64, 192).astype(jnp.int32),
        "weights": scatter_about(key_list[3], (NASSET, PORT), 0.25, 1.5, ((0, 32),)),
    }


def reference(returns, start_day, shrink_code, weights):
    days = jnp.arange(TDAY, dtype=jnp.int32)
    listed = days[None, :] >= start_day[:, None]
    masked = jnp.where(listed, returns, jnp.zeros_like(returns)).astype(jnp.bfloat16)
    observed = (masked != 0).astype(jnp.bfloat16)
    squared = (masked.astype(jnp.float32) * masked.astype(jnp.float32)).astype(jnp.bfloat16)
    counts = lax.optimization_barrier(jnp.sum(observed.astype(jnp.float32), axis=1))
    sigma = jnp.sqrt(lax.optimization_barrier(jnp.sum(squared.astype(jnp.float32), axis=1)) / jnp.maximum(counts, 1.0) + 1e-06)
    scaled = (sigma[:, None] * weights.astype(jnp.float32)).astype(jnp.bfloat16)
    delta = shrink_code[0].astype(jnp.float32) / DENOM
    block_rows = math.gcd(NASSET, 512)
    col_ids = jnp.arange(NASSET, dtype=jnp.int32)

    def one_block(index):
        first = (index * block_rows).astype(jnp.int32)
        rows_y = lax.dynamic_slice_in_dim(masked, first, block_rows, 0)
        rows_o = lax.dynamic_slice_in_dim(observed, first, block_rows, 0)
        rows_s = lax.dynamic_slice_in_dim(squared, first, block_rows, 0)
        cross = jnp.dot(rows_y, masked.T, preferred_element_type=jnp.float32)
        left = jnp.dot(rows_s, observed.T, preferred_element_type=jnp.float32)
        right = jnp.dot(rows_o, squared.T, preferred_element_type=jnp.float32)
        corr = cross / jnp.sqrt(left * right + 1e-06)
        row_ids = first + jnp.arange(block_rows, dtype=jnp.int32)
        ident = (row_ids[:, None] == col_ids[None, :]).astype(jnp.float32)
        shrunk = ((1.0 - delta) * corr + delta * ident).astype(jnp.bfloat16)
        row_sigma = lax.dynamic_slice_in_dim(sigma, first, block_rows, 0)
        return row_sigma[:, None] * jnp.dot(shrunk, scaled, preferred_element_type=jnp.float32)
    blocks = lax.map(one_block, jnp.arange(NASSET // block_rows, dtype=jnp.int32))
    return blocks.reshape(NASSET, PORT)
```

```python
import functools

import jax
import jax.numpy as jnp
from jax import lax
from jax.experimental import pallas as pl
from jax.experimental.pallas import tpu as pltpu
from jax.sharding import PartitionSpec as P

DENOM = 256
VMEM = pltpu.VMEM


def vspec():
    return pl.BlockSpec(memory_space=VMEM)


def prep_kernel(start_ref, ret_ref, w_ref, masked_ref, both_ref, sigma_ref):
    rows, days = ret_ref.shape
    start = jnp.broadcast_to(start_ref[...].astype(jnp.float32), (days, rows)).T
    day = lax.broadcasted_iota(jnp.int32, (rows, days), 1).astype(jnp.float32)
    y = jnp.where(day >= start, ret_ref[...].astype(jnp.float32), 0.0)
    masked_ref[...] = y.astype(jnp.bfloat16)
    both_ref[:, :days] = y.astype(jnp.bfloat16)
    sq = (y * y).astype(jnp.bfloat16).astype(jnp.float32)
    obs = jnp.where(y != 0.0, 1.0, 0.0)
    total = jnp.sum(sq, axis=1, keepdims=True)
    count = jnp.sum(obs, axis=1, keepdims=True)
    sigma = jnp.sqrt(total / jnp.maximum(count, 1.0) + 1e-06)
    sigma_ref[...] = jnp.broadcast_to(sigma, sigma_ref.shape)
    both_ref[:, days:] = (sigma * w_ref[...].astype(jnp.float32)).astype(jnp.bfloat16)


def nt(a, b):
    return lax.dot_general(a, b, (((1,), (1,)), ((), ())), preferred_element_type=jnp.float32)


def parts_of(y):
    wide = y.astype(jnp.float32)
    obs = jnp.where(wide != 0.0, 1.0, 0.0).astype(jnp.bfloat16)
    return y, obs, (wide * wide).astype(jnp.bfloat16)


def corr_kernel(nrows, has_diag, code_ref, *refs):
    row_refs, col_refs, out_ref = refs[:nrows], refs[nrows:-1], refs[-1]
    own, days = row_refs[0].shape
    delta = code_ref[0].astype(jnp.float32) / DENOM
    keep = 1.0 - delta
    cols = [parts_of(c[:, :days]) for c in col_refs]
    for i, r in enumerate(row_refs):
        ry, ro, rs = parts_of(r[...])
        for j, (cy, co, cs) in enumerate(cols):
            cross, left, right = nt(ry, cy), nt(rs, co), nt(ro, cs)
            shrunk = keep * (cross * lax.rsqrt(left * right + 1e-06))
            if has_diag and i == 0 and j == 0:
                a = lax.broadcasted_iota(jnp.int32, shrunk.shape, 0)
                b = lax.broadcasted_iota(jnp.int32, shrunk.shape, 1)
                shrunk = shrunk + jnp.where(a == b, delta, 0.0)
            out_ref[i * own:(i + 1) * own, j * own:(j + 1) * own] = shrunk.astype(jnp.bfloat16)


def apply_kernel(nchunk, ncore, days, *refs):
    s_refs, v_refs, out_ref = refs[:nchunk], refs[nchunk:-1], refs[-1]
    acc = None
    for k in range(nchunk):
        own = v_refs[0].shape[0]
        for j in range(ncore):
            term = jnp.dot(
                s_refs[k][:, j * own:(j + 1) * own],
                v_refs[k * ncore + j][:, days:],
                preferred_element_type=jnp.float32,
            )
            acc = term if acc is None else acc + term
    out_ref[...] = acc.astype(out_ref.dtype)


def final_kernel(sigma_ref, own_ref, *refs):
    out_ref = refs[-1]
    total = own_ref[...]
    for r in refs[:-1]:
        total = total + r[...].astype(jnp.float32)
    out_ref[...] = sigma_ref[:, :1] * total


def call(kernel, args, outs, specs=None, grid=()):
    return pl.pallas_call(
        kernel,
        grid=grid,
        out_shape=outs,
        in_specs=specs or [vspec() for _ in args],
        out_specs=jax.tree.map(lambda _: vspec(), outs),
        compiler_params=pltpu.CompilerParams(vmem_limit_bytes=48 * 1024 * 1024),
    )(*args)


def per_device(nrow, ncol, returns, start_day, shrink_code, weights):
    own, days = returns.shape
    ports = weights.shape[1]
    far_y, far_z = nrow // 2, ncol // 4

    def send(value, y=0, x=0, zh=0, zl=0, core=0):
        pairs = []
        for r in range(nrow):
            for c in range(ncol):
                rr = (r // 2 + y) % far_y * 2 + (r % 2 + x) % 2
                cc = (c // 4 + zh) % far_z * 4 + (c // 2 % 2 + zl) % 2 * 2 + (c % 2 + core) % 2
                pairs.append((r * ncol + c, rr * ncol + cc))
        return lax.ppermute(value, ("row", "col"), pairs)

    masked, both, sigma = call(
        prep_kernel,
        (start_day.reshape(1, own), returns, weights),
        (
            jax.ShapeDtypeStruct((own, days), jnp.bfloat16),
            jax.ShapeDtypeStruct((own, days + ports), jnp.bfloat16),
            jax.ShapeDtypeStruct((own, 128), jnp.float32),
        ),
    )
    square = [(x, zl) for x in range(2) for zl in range(2)]
    chips = {(0, 0): both}
    for zh in range(1, far_z):
        chips[zh, 0] = send(both, zh=zh)
    for y in range(1, far_y):
        chips[0, y] = send(both, y=y)
    rows = [masked] + [send(masked, x=x, zl=zl) for x, zl in square[1:]]
    for zh in range(1, far_z):
        for y in range(1, far_y):
            chips[zh, y] = send(chips[zh, 0], y=y)
    order = sorted(chips, key=lambda k: (k[0] > 0 and k[1] > 0, k[0] > 0, k))
    swapped = {k: send(chips[k], core=1) for k in order}

    smem = pl.BlockSpec(memory_space=pltpu.SMEM)
    blocks = []
    for k in order:
        args = (shrink_code, *rows, chips[k], swapped[k])
        blocks.append(call(
            functools.partial(corr_kernel, len(rows), k == (0, 0)),
            args,
            jax.ShapeDtypeStruct((len(rows) * own, 2 * own), jnp.bfloat16),
            [smem] + [vspec() for _ in args[1:]],
        ))
    values = [v for k in order for v in (chips[k], swapped[k])]

    def partial_of(i, dtype):
        piece = pl.BlockSpec((own, 2 * own), lambda g: (i, 0))
        return call(
            functools.partial(apply_kernel, len(order), 2, days),
            (*blocks, *values),
            jax.ShapeDtypeStruct((own, ports), dtype),
            [piece for _ in blocks] + [vspec() for _ in values],
            (1,),
        )

    arrived = []
    for i in (3, 1, 2):
        x, zl = square[i]
        arrived.append(send(partial_of(i, jnp.bfloat16), x=x, zl=zl))
    mine = partial_of(0, jnp.float32)
    return call(
        final_kernel, (sigma, mine, *arrived), jax.ShapeDtypeStruct((own, ports), jnp.float32)
    )


def solution(mesh):
    in_specs = (P(("col", "row"), None), P(("col", "row")), P(), P(("col", "row"), None))
    out_specs = P(("col", "row"), None)
    body = functools.partial(per_device, mesh.shape["row"], mesh.shape["col"])
    return jax.shard_map(
        body, mesh=mesh, in_specs=in_specs, out_specs=out_specs, check_vma=False
    )
```

```python
import functools

import jax
import jax.numpy as jnp
from jax import lax
from jax.experimental import pallas as pl
from jax.experimental.pallas import tpu as pltpu
from jax.sharding import PartitionSpec as P

DENOM = 256
VMEM = pltpu.VMEM


def vspec():
    return pl.BlockSpec(memory_space=VMEM)


def prep_kernel(start_hbm, ret_hbm, w_hbm, *refs):
    masked_ref, both_ref, sigma_ref, *piece_refs = refs[:-4]
    start_ref, ret_ref, w_ref, sems = refs[-4:]
    loads = [
        pltpu.make_async_copy(src, dst, sems.at[k])
        for k, (src, dst) in enumerate(((start_hbm, start_ref), (ret_hbm, ret_ref), (w_hbm, w_ref)))
    ]
    for load in loads:
        load.start()
    rows, days = ret_ref.shape
    loads[0].wait()
    loads[1].wait()
    start = jnp.broadcast_to(start_ref[...].astype(jnp.float32), (days, rows)).T
    day = lax.broadcasted_iota(jnp.int32, (rows, days), 1).astype(jnp.float32)
    y = jnp.where(day >= start, ret_ref[...].astype(jnp.float32), 0.0)
    sq = (y * y).astype(jnp.bfloat16).astype(jnp.float32)
    obs = jnp.where(y != 0.0, 1.0, 0.0)
    total = jnp.sum(sq, axis=1, keepdims=True)
    count = jnp.sum(obs, axis=1, keepdims=True)
    sigma = jnp.sqrt(total / jnp.maximum(count, 1.0) + 1e-06)
    sigma_ref[...] = jnp.broadcast_to(sigma, sigma_ref.shape)
    masked = y.astype(jnp.bfloat16)
    loads[2].wait()
    scaled = (sigma * w_ref[...].astype(jnp.float32)).astype(jnp.bfloat16)
    masked_ref[...] = masked
    both_ref[:, :days] = masked
    both_ref[:, days:] = scaled
    at = 0
    for ref in piece_refs:
        end = at + ref.shape[0]
        ref[:, :days] = masked[at:end]
        ref[:, days:] = scaled[at:end]
        at = end % rows


def nt(a, b):
    return lax.dot_general(a, b, (((1,), (1,)), ((), ())), preferred_element_type=jnp.float32)


def parts_of(y):
    wide = y.astype(jnp.float32)
    obs = jnp.where(wide != 0.0, 1.0, 0.0).astype(jnp.bfloat16)
    return y, obs, (wide * wide).astype(jnp.bfloat16)


def chip_kernel(nrows, ncols, nin, has_diag, code_ref, *refs):
    row_refs, col_refs = refs[:nrows], refs[nrows:nrows + ncols]
    in_refs, out_refs = refs[nrows + ncols:nrows + ncols + nin], refs[nrows + ncols + nin:]
    days = row_refs[0].shape[1]
    own = out_refs[0].shape[0]
    delta = code_ref[0].astype(jnp.float32) / DENOM
    keep = 1.0 - delta
    ys, values = [c[:, :days] for c in col_refs], [c[:, days:] for c in col_refs]
    while len(ys) > 1 and sum(y.shape[0] for y in ys[:2]) <= own:
        ys = [jnp.concatenate(ys[k:k + 2]) for k in range(0, len(ys), 2)]
    cols = [parts_of(y) for y in ys]
    values = jnp.concatenate(values)
    tiles = [r[t * own:(t + 1) * own] for r in row_refs for t in range(r.shape[0] // own)]
    for i, tile in enumerate(tiles):
        ry, ro, rs = parts_of(tile)
        shrunk = []
        for j, (cy, co, cs) in enumerate(cols):
            cross, left, right = nt(ry, cy), nt(rs, co), nt(ro, cs)
            part = keep * (cross * lax.rsqrt(left * right + 1e-06))
            if has_diag and i == 0 and j == 0:
                a = lax.broadcasted_iota(jnp.int32, part.shape, 0)
                b = lax.broadcasted_iota(jnp.int32, part.shape, 1)
                part = part + jnp.where(a == b, delta, 0.0)
            shrunk.append(part.astype(jnp.bfloat16))
        term = jnp.dot(jnp.concatenate(shrunk, 1), values, preferred_element_type=jnp.float32)
        if nin:
            term = term + in_refs[i][...]
        out_refs[i][...] = term.astype(out_refs[i].dtype)


def final_kernel(sigma_ref, *refs):
    out_ref = refs[-1]
    total = refs[0][...]
    for r in refs[1:-1]:
        total = total + r[...].astype(jnp.float32)
    out_ref[...] = sigma_ref[:, :1] * total


def join_kernel(a_ref, b_ref, out_ref):
    n = a_ref.shape[0]
    out_ref[:n] = a_ref[...]
    out_ref[n:] = b_ref[...]


def call(kernel, args, outs, specs=None, scratch=(), aliases=None):
    return pl.pallas_call(
        kernel,
        out_shape=outs,
        in_specs=specs or [vspec() for _ in args],
        out_specs=jax.tree.map(lambda _: vspec(), outs),
        scratch_shapes=scratch,
        input_output_aliases=aliases or {},
        compiler_params=pltpu.CompilerParams(vmem_limit_bytes=48 * 1024 * 1024),
    )(*args)


def after(value, *others):
    return lax.optimization_barrier((value, *others))[0]


def per_device(nrow, ncol, returns, start_day, shrink_code, weights):
    own, days = returns.shape
    ports = weights.shape[1]
    cut = own // 2
    far_y, far_z = nrow // 2, ncol // 4

    def send(value, y=0, x=0, zh=0, zl=0, core=0):
        pairs = []
        for r in range(nrow):
            for c in range(ncol):
                rr = (r // 2 + y) % far_y * 2 + (r % 2 + x) % 2
                cc = (c // 4 + zh) % far_z * 4 + (c // 2 % 2 + zl) % 2 * 2 + (c % 2 + core) % 2
                pairs.append((r * ncol + c, rr * ncol + cc))
        return lax.ppermute(value, ("row", "col"), pairs)

    smem = pl.BlockSpec(memory_space=pltpu.SMEM)
    shape = jax.ShapeDtypeStruct
    masked, both, sigma, low, high = call(
        prep_kernel,
        tuple(
            pltpu.with_memory_space_constraint(v, pltpu.HBM)
            for v in (start_day.reshape(1, own), returns, weights)
        ),
        (
            shape((own, days), jnp.bfloat16),
            shape((own, days + ports), jnp.bfloat16),
            shape((own, 128), jnp.float32),
            *(shape((n, days + ports), jnp.bfloat16) for n in (cut, own - cut)),
        ),
        [pl.BlockSpec(memory_space=pltpu.HBM)] * 3,
        [
            VMEM((1, own), jnp.int32),
            VMEM((own, days), jnp.bfloat16),
            VMEM((own, ports), jnp.bfloat16),
            pltpu.SemaphoreType.DMA((3,)),
        ],
    )
    far_low = {zh: send(low, zh=zh) for zh in range(1, far_z)}
    far_high = {zh: send(high, zh=zh) for zh in range(1, far_z)}
    near = {y: send(both, y=y) for y in range(1, far_y)}
    from_x = send(masked, x=1)
    from_z = send(masked, zl=1)
    from_xz = send(from_x, zl=1)
    rows = [masked, from_x, from_z, from_xz]
    gate = [from_z, from_xz, *far_low.values()]
    rows[2:] = [after(v, *gate) for v in rows[2:]]
    far_low = {zh: after(v, *gate) for zh, v in far_low.items()}
    total = []

    def chip(cols, last=False):
        args = (shrink_code, *rows, *cols, *total)
        nin = len(total)
        kinds = [jnp.float32] + [jnp.bfloat16 if last else jnp.float32] * 3
        total[:] = call(
            functools.partial(chip_kernel, len(rows), len(cols), nin, nin == 0),
            args,
            [VMEM((own, ports), kind) for kind in kinds],
            [smem] + [vspec() for _ in args[1:]],
            aliases={len(args) - nin + i: i for i in range(nin)} if not last else None,
        )

    pass_low = [send(v, y=y) for v in far_low.values() for y in near]
    low_swap = [send(v, core=1) for v in far_low.values()]
    far_high = {zh: after(v, *low_swap) for zh, v in far_high.items()}
    hold = list(far_high.values())
    pass_high = [send(v, y=y) for v in far_high.values() for y in near]
    high_swap = [send(v, core=1) for v in far_high.values()]
    own_swap = send(after(both, *hold), core=1)
    near = {y: after(v, *hold) for y, v in near.items()}
    near_swap = [send(v, core=1) for v in near.values()]
    chip([both, own_swap])
    for pair in zip(near.values(), near_swap):
        chip(pair)
    for four in zip(far_low.values(), far_high.values(), low_swap, high_swap):
        chip(four)
    pass_low = [after(v, *total) for v in pass_low]
    pass_high = [after(v, *total) for v in pass_high]
    low_swap = [send(v, core=1) for v in pass_low]
    high_swap = [send(v, core=1) for v in pass_high]
    tail = list(zip(pass_low, pass_high, low_swap, high_swap))
    for k, four in enumerate(tail):
        chip(four, k == len(tail) - 1)

    arrived = [total[0]]
    for i, x, zl in ((3, 1, 1), (1, 1, 0), (2, 0, 1)):
        arrived.append(send(total[i], x=x, zl=zl))
    return call(final_kernel, (sigma, *arrived), shape((own, ports), jnp.float32))


def solution(mesh):
    in_specs = (P(("col", "row"), None), P(("col", "row")), P(), P(("col", "row"), None))
    out_specs = P(("col", "row"), None)
    body = functools.partial(per_device, mesh.shape["row"], mesh.shape["col"])
    return jax.shard_map(
        body, mesh=mesh, in_specs=in_specs, out_specs=out_specs, check_vma=False
    )
```

```python
import functools

import jax
import jax.numpy as jnp
from jax import lax
from jax.experimental import pallas as pl
from jax.experimental.pallas import tpu as pltpu
from jax.sharding import PartitionSpec as P

DENOM = 256
VMEM = pltpu.VMEM


def vspec():
    return pl.BlockSpec(memory_space=VMEM)


def prep_kernel(start_hbm, ret_hbm, w_hbm, *refs):
    masked_ref, both_ref, sigma_ref, start_ref, ret_ref, w_ref, sems = refs
    loads = [
        pltpu.make_async_copy(src, dst, sems.at[k])
        for k, (src, dst) in enumerate(((start_hbm, start_ref), (ret_hbm, ret_ref), (w_hbm, w_ref)))
    ]
    for load in loads:
        load.start()
    rows, days = ret_ref.shape
    loads[0].wait()
    loads[1].wait()
    start = jnp.broadcast_to(start_ref[...].astype(jnp.float32), (days, rows)).T
    day = lax.broadcasted_iota(jnp.int32, (rows, days), 1).astype(jnp.float32)
    y = jnp.where(day >= start, ret_ref[...].astype(jnp.float32), 0.0)
    sigma = sigma_of(y)
    sigma_ref[...] = jnp.broadcast_to(sigma, sigma_ref.shape)
    masked = y.astype(jnp.bfloat16)
    masked_ref[...] = masked
    both_ref[:, :days] = masked
    loads[2].wait()
    both_ref[:, days:] = (sigma * w_ref[...].astype(jnp.float32)).astype(jnp.bfloat16)


def sigma_of(y):
    sq = (y * y).astype(jnp.bfloat16).astype(jnp.float32)
    obs = jnp.where(y != 0.0, 1.0, 0.0)
    total = jnp.sum(sq, axis=1, keepdims=True)
    count = jnp.sum(obs, axis=1, keepdims=True)
    return jnp.sqrt(total / jnp.maximum(count, 1.0) + 1e-06)


def nt(a, b):
    return lax.dot_general(a, b, (((1,), (1,)), ((), ())), preferred_element_type=jnp.float32)


def parts_of(y):
    wide = y.astype(jnp.float32)
    obs = jnp.where(wide != 0.0, 1.0, 0.0).astype(jnp.bfloat16)
    return y, obs, (wide * wide).astype(jnp.bfloat16)


def chip_kernel(nrows, pairs, nin, has_diag, code_ref, *refs):
    ncols = sum(pairs)
    row_refs, col_refs = refs[:nrows], refs[nrows:nrows + ncols]
    in_refs, out_refs = refs[nrows + ncols:nrows + ncols + nin], refs[nrows + ncols + nin:]
    own, days = row_refs[0].shape
    delta = code_ref[0].astype(jnp.float32) / DENOM
    keep = 1.0 - delta
    ys, values, at = [], [], 0
    for n in pairs:
        if n == 1:
            ys.append(col_refs[at][:, :days])
            values.append(col_refs[at][:, days:])
        else:
            y = col_refs[at][...]
            ys.append(y)
            sigma = sigma_of(y.astype(jnp.float32))
            values.append((sigma * col_refs[at + 1][...].astype(jnp.float32)).astype(jnp.bfloat16))
        at += n
    cols = [parts_of(y) for y in ys]
    values = jnp.concatenate(values)
    for i, r in enumerate(row_refs):
        ry, ro, rs = parts_of(r[...])
        shrunk = []
        for j, (cy, co, cs) in enumerate(cols):
            cross, left, right = nt(ry, cy), nt(rs, co), nt(ro, cs)
            part = keep * (cross * lax.rsqrt(left * right + 1e-06))
            if has_diag and i == 0 and j == 0:
                a = lax.broadcasted_iota(jnp.int32, part.shape, 0)
                b = lax.broadcasted_iota(jnp.int32, part.shape, 1)
                part = part + jnp.where(a == b, delta, 0.0)
            shrunk.append(part.astype(jnp.bfloat16))
        term = jnp.dot(jnp.concatenate(shrunk, 1), values, preferred_element_type=jnp.float32)
        if nin:
            term = term + in_refs[i][...]
        out_refs[i][...] = term.astype(out_refs[i].dtype)


def final_kernel(sigma_ref, *refs):
    out_ref = refs[-1]
    total = refs[0][...]
    for r in refs[1:-1]:
        total = total + r[...].astype(jnp.float32)
    out_ref[...] = sigma_ref[:, :1] * total


def call(kernel, args, outs, specs=None, scratch=(), aliases=None):
    return pl.pallas_call(
        kernel,
        out_shape=outs,
        in_specs=specs or [vspec() for _ in args],
        out_specs=jax.tree.map(lambda _: vspec(), outs),
        scratch_shapes=scratch,
        input_output_aliases=aliases or {},
        compiler_params=pltpu.CompilerParams(vmem_limit_bytes=48 * 1024 * 1024),
    )(*args)


def after(value, *others):
    return lax.optimization_barrier((value, *others))[0]


def per_device(nrow, ncol, returns, start_day, shrink_code, weights):
    own, days = returns.shape
    ports = weights.shape[1]
    far_y, far_z = nrow // 2, ncol // 4
    ys, zs = range(1, far_y), range(1, far_z)

    def send(value, y=0, x=0, zh=0, zl=0, core=0):
        pairs = []
        for r in range(nrow):
            for c in range(ncol):
                rr = (r // 2 + y) % far_y * 2 + (r % 2 + x) % 2
                cc = (c // 4 + zh) % far_z * 4 + (c // 2 % 2 + zl) % 2 * 2 + (c % 2 + core) % 2
                pairs.append((r * ncol + c, rr * ncol + cc))
        return lax.ppermute(value, ("row", "col"), pairs)

    smem = pl.BlockSpec(memory_space=pltpu.SMEM)
    shape = jax.ShapeDtypeStruct
    masked, both, sigma = call(
        prep_kernel,
        tuple(
            pltpu.with_memory_space_constraint(v, pltpu.HBM)
            for v in (start_day.reshape(1, own), returns, weights)
        ),
        (
            shape((own, days), jnp.bfloat16),
            shape((own, days + ports), jnp.bfloat16),
            shape((own, 128), jnp.float32),
        ),
        [pl.BlockSpec(memory_space=pltpu.HBM)] * 3,
        [
            VMEM((1, own), jnp.int32),
            VMEM((own, days), jnp.bfloat16),
            VMEM((own, ports), jnp.bfloat16),
            pltpu.SemaphoreType.DMA((3,)),
        ],
    )
    total, rows = [], []

    def chip(*pieces, last=False):
        args = (shrink_code, *rows, *(a for p in pieces for a in p), *total)
        nin = len(total)
        kinds = [jnp.float32] + [jnp.bfloat16 if last else jnp.float32] * 3
        total[:] = call(
            functools.partial(chip_kernel, len(rows), tuple(map(len, pieces)), nin, nin == 0),
            args,
            [VMEM((own, ports), kind) for kind in kinds],
            [smem] + [vspec() for _ in args[1:]],
            aliases={len(args) - nin + i: i for i in range(nin)} if not last else None,
        )
        return list(total)

    at = {}
    at["zl"] = [send(masked, zl=1)]
    at["zh_m"] = [send(masked, zh=k) for k in zs]
    at["xzl"] = [send(masked, x=1, zl=1)]
    at["own_s"] = [send(both, core=1)]
    at["zh_w"] = [send(weights, zh=k) for k in zs]
    at["fwd_w"] = [send(after(v, *at["xzl"]), y=k) for v in at["zh_w"] for k in ys]
    at["w_s"] = [send(v, core=1) for v in at["zh_w"]]
    at["x"] = [send(masked, x=1)]
    at["near"] = [send(both, y=k) for k in ys]
    at["near_s"] = [send(after(v, *at["zl"]), core=1) for v in at["near"]]
    at["fwd_m"] = [send(after(v, *at["near_s"], *at["w_s"]), y=k) for v in at["zh_m"] for k in ys]
    rows += [masked, at["x"][0], at["zl"][0], at["xzl"][0]]
    at["K1"] = chip((both,), (at["own_s"][0],))
    for a, b in zip(at["near"], at["near_s"]):
        at["K2"] = chip((after(a, *at["zh_m"]),), (b,))
    at["m_s"] = [send(after(v, *at["K1"]), core=1) for v in at["zh_m"]]
    for a, b, p, q in zip(at["zh_m"], at["zh_w"], at["m_s"], at["w_s"]):
        at["K3"] = chip((a, b), (p, q))
    at["fw_s"] = [send(after(v, *at["m_s"], *at["K3"], *at["zh_m"]), core=1) for v in at["fwd_w"]]
    at["fm_s"] = [send(after(v, *at["K3"]), core=1) for v in at["fwd_m"]]
    tail = list(zip(at["fwd_m"], at["fwd_w"], at["fm_s"], at["fw_s"]))
    for k, (a, b, p, q) in enumerate(tail):
        chip((a, b), (p, q), last=k == len(tail) - 1)

    arrived = [total[0]]
    for i, x, zl in ((3, 1, 1), (1, 1, 0), (2, 0, 1)):
        arrived.append(send(total[i], x=x, zl=zl))
    return call(final_kernel, (sigma, *arrived), shape((own, ports), jnp.float32))


def solution(mesh):
    in_specs = (P(("col", "row"), None), P(("col", "row")), P(), P(("col", "row"), None))
    out_specs = P(("col", "row"), None)
    body = functools.partial(per_device, mesh.shape["row"], mesh.shape["col"])
    return jax.shard_map(
        body, mesh=mesh, in_specs=in_specs, out_specs=out_specs, check_vma=False
    )
```

```python
import functools

import jax
import jax.numpy as jnp
from jax import lax
from jax.experimental import pallas as pl
from jax.experimental.pallas import tpu as pltpu
from jax.sharding import PartitionSpec as P

DENOM = 256
VMEM = pltpu.VMEM


def vspec():
    return pl.BlockSpec(memory_space=VMEM)


def prep_kernel(start_hbm, ret_hbm, w_hbm, *refs):
    masked_ref, both_ref, sigma_ref, start_ref, ret_ref, w_ref, sems = refs
    loads = [
        pltpu.make_async_copy(src, dst, sems.at[k])
        for k, (src, dst) in enumerate(((start_hbm, start_ref), (ret_hbm, ret_ref), (w_hbm, w_ref)))
    ]
    for load in loads:
        load.start()
    rows, days = ret_ref.shape
    loads[0].wait()
    loads[1].wait()
    start = jnp.broadcast_to(start_ref[...].astype(jnp.float32), (days, rows)).T
    day = lax.broadcasted_iota(jnp.int32, (rows, days), 1).astype(jnp.float32)
    y = jnp.where(day >= start, ret_ref[...].astype(jnp.float32), 0.0)
    sigma = sigma_of(y)
    sigma_ref[...] = jnp.broadcast_to(sigma, sigma_ref.shape)
    masked = y.astype(jnp.bfloat16)
    masked_ref[...] = masked
    both_ref[:, :days] = masked
    loads[2].wait()
    both_ref[:, days:] = (sigma * w_ref[...].astype(jnp.float32)).astype(jnp.bfloat16)


def sigma_of(y):
    sq = (y * y).astype(jnp.bfloat16).astype(jnp.float32)
    obs = jnp.where(y != 0.0, 1.0, 0.0)
    total = jnp.sum(sq, axis=1, keepdims=True)
    count = jnp.sum(obs, axis=1, keepdims=True)
    return jnp.sqrt(total / jnp.maximum(count, 1.0) + 1e-06)


def nt(a, b):
    return lax.dot_general(a, b, (((1,), (1,)), ((), ())), preferred_element_type=jnp.float32)


def parts_of(y):
    wide = y.astype(jnp.float32)
    obs = jnp.where(wide != 0.0, 1.0, 0.0).astype(jnp.bfloat16)
    return y, obs, (wide * wide).astype(jnp.bfloat16)


def chip_kernel(nrows, pairs, nin, has_diag, code_ref, *refs):
    ncols = sum(pairs)
    row_refs, col_refs = refs[:nrows], refs[nrows:nrows + ncols]
    in_refs, out_refs = refs[nrows + ncols:nrows + ncols + nin], refs[nrows + ncols + nin:]
    own, days = row_refs[0].shape
    delta = code_ref[0].astype(jnp.float32) / DENOM
    keep = 1.0 - delta
    ys, values, at = [], [], 0
    for n in pairs:
        if n == 1:
            ys.append(col_refs[at][:, :days])
            values.append(col_refs[at][:, days:])
        else:
            y = col_refs[at][...]
            ys.append(y)
            sigma = sigma_of(y.astype(jnp.float32))
            values.append((sigma * col_refs[at + 1][...].astype(jnp.float32)).astype(jnp.bfloat16))
        at += n
    cols = [parts_of(y) for y in ys]
    values = jnp.concatenate(values)
    for i, r in enumerate(row_refs):
        ry, ro, rs = parts_of(r[...])
        shrunk = []
        for j, (cy, co, cs) in enumerate(cols):
            cross, left, right = nt(ry, cy), nt(rs, co), nt(ro, cs)
            part = keep * (cross * lax.rsqrt(left * right + 1e-06))
            if has_diag and i == 0 and j == 0:
                a = lax.broadcasted_iota(jnp.int32, part.shape, 0)
                b = lax.broadcasted_iota(jnp.int32, part.shape, 1)
                part = part + jnp.where(a == b, delta, 0.0)
            shrunk.append(part.astype(jnp.bfloat16))
        term = jnp.dot(jnp.concatenate(shrunk, 1), values, preferred_element_type=jnp.float32)
        if nin:
            term = term + in_refs[i][...]
        out_refs[i][...] = term.astype(out_refs[i].dtype)


def final_kernel(sigma_ref, *refs):
    out_ref = refs[-1]
    total = refs[0][...]
    for r in refs[1:-1]:
        total = total + r[...].astype(jnp.float32)
    out_ref[...] = sigma_ref[:, :1] * total


def call(kernel, args, outs, specs=None, scratch=(), aliases=None):
    return pl.pallas_call(
        kernel,
        out_shape=outs,
        in_specs=specs or [vspec() for _ in args],
        out_specs=jax.tree.map(lambda _: vspec(), outs),
        scratch_shapes=scratch,
        input_output_aliases=aliases or {},
        compiler_params=pltpu.CompilerParams(vmem_limit_bytes=48 * 1024 * 1024),
    )(*args)


def after(value, *others):
    return lax.optimization_barrier((value, *others))[0]


def per_device(nrow, ncol, returns, start_day, shrink_code, weights):
    own, days = returns.shape
    ports = weights.shape[1]
    far_y, far_z = nrow // 2, ncol // 4
    ys, zs = range(1, far_y), range(1, far_z)

    def send(value, y=0, x=0, zh=0, zl=0, core=0):
        pairs = []
        for r in range(nrow):
            for c in range(ncol):
                rr = (r // 2 + y) % far_y * 2 + (r % 2 + x) % 2
                cc = (c // 4 + zh) % far_z * 4 + (c // 2 % 2 + zl) % 2 * 2 + (c % 2 + core) % 2
                pairs.append((r * ncol + c, rr * ncol + cc))
        return lax.ppermute(value, ("row", "col"), pairs)

    smem = pl.BlockSpec(memory_space=pltpu.SMEM)
    shape = jax.ShapeDtypeStruct
    masked, both, sigma = call(
        prep_kernel,
        tuple(
            pltpu.with_memory_space_constraint(v, pltpu.HBM)
            for v in (start_day.reshape(1, own), returns, weights)
        ),
        (
            shape((own, days), jnp.bfloat16),
            shape((own, days + ports), jnp.bfloat16),
            shape((own, 128), jnp.float32),
        ),
        [pl.BlockSpec(memory_space=pltpu.HBM)] * 3,
        [
            VMEM((1, own), jnp.int32),
            VMEM((own, days), jnp.bfloat16),
            VMEM((own, ports), jnp.bfloat16),
            pltpu.SemaphoreType.DMA((3,)),
        ],
    )
    total, rows = [], []

    def chip(*pieces, last=False):
        first = not total
        new = {}
        for part in ((3,), (1, 2, 0)) if last else (range(4),):
            into = [] if first else [total[i] for i in part]
            args = (shrink_code, *(rows[i] for i in part), *(a for p in pieces for a in p), *into)
            kinds = [jnp.bfloat16 if last and i else jnp.float32 for i in part]
            made = call(
                functools.partial(chip_kernel, len(part), tuple(map(len, pieces)), len(into), first),
                args,
                [VMEM((own, ports), kind) for kind in kinds],
                [smem] + [vspec() for _ in args[1:]],
                aliases=None if last else {len(args) - len(into) + k: k for k in range(len(into))},
            )
            new.update(zip(part, made))
        total[:] = [new[i] for i in range(4)]
        return list(total)

    at = {}
    at["zh_w"] = [send(weights, zh=k) for k in zs]
    at["zh_m"] = [send(masked, zh=k) for k in zs]
    at["near_w"] = [send(weights, y=k) for k in ys]
    at["near_m"] = [send(masked, y=k) for k in ys]
    at["fwd_w"] = [send(v, y=k) for v in at["zh_w"] for k in ys]
    at["m_s"] = [send(v, core=1) for v in at["zh_m"]]
    at["w_s"] = [send(after(v, *at["zh_m"]), core=1) for v in at["zh_w"]]
    at["nw_s"] = [send(v, core=1) for v in at["near_w"]]
    at["zl"] = [send(masked, zl=1)]
    at["x"] = [send(after(masked, *at["zl"]), x=1)]
    at["own_s"] = [send(after(both, *at["near_m"], *at["zl"]), core=1)]
    at["xzl"] = [send(at["x"][0], zl=1)]
    at["nm_s"] = [send(after(v, *at["zl"]), core=1) for v in at["near_m"]]
    at["fwd_m"] = [send(after(v, *at["xzl"]), y=k) for v in at["zh_m"] for k in ys]
    rows += [masked, at["x"][0], at["zl"][0], at["xzl"][0]]
    at["K1"] = chip((after(both, *at["zh_w"]),), (at["own_s"][0],), *zip((*at["near_m"], *at["nm_s"]), (*at["near_w"], *at["nw_s"])))
    at["K2"] = at["K1"]
    at["fw_s"] = [send(v, core=1) for v in at["fwd_w"]]
    for a, b, p, q in zip(at["zh_m"], at["zh_w"], at["m_s"], at["w_s"]):
        at["K3"] = chip((a, b), (p, q))
    at["fm_s"] = [send(after(v, *at["K2"]), core=1) for v in at["fwd_m"]]
    tail = list(zip(at["fwd_m"], at["fwd_w"], at["fm_s"], at["fw_s"]))
    for k, (a, b, p, q) in enumerate(tail):
        chip((a, b), (p, q), last=k == len(tail) - 1)

    arrived = [total[0]]
    for i, x, zl in ((3, 1, 1), (1, 1, 0), (2, 0, 1)):
        arrived.append(send(total[i], x=x, zl=zl))
    return call(final_kernel, (sigma, *arrived), shape((own, ports), jnp.float32))


def solution(mesh):
    in_specs = (P(("col", "row"), None), P(("col", "row")), P(), P(("col", "row"), None))
    out_specs = P(("col", "row"), None)
    body = functools.partial(per_device, mesh.shape["row"], mesh.shape["col"])
    return jax.shard_map(
        body, mesh=mesh, in_specs=in_specs, out_specs=out_specs, check_vma=False
    )
```

```python
import functools

import jax
import jax.numpy as jnp
from jax import lax
from jax.experimental import pallas as pl
from jax.experimental.pallas import tpu as pltpu
from jax.sharding import PartitionSpec as P

DENOM = 256
VMEM = pltpu.VMEM


def vspec():
    return pl.BlockSpec(memory_space=VMEM)


def prep_kernel(start_hbm, ret_hbm, w_hbm, *refs):
    masked_ref, both_ref, sigma_ref, start_ref, ret_ref, w_ref, sems = refs
    loads = [
        pltpu.make_async_copy(src, dst, sems.at[k])
        for k, (src, dst) in enumerate(((start_hbm, start_ref), (ret_hbm, ret_ref), (w_hbm, w_ref)))
    ]
    for load in loads:
        load.start()
    rows, days = ret_ref.shape
    loads[0].wait()
    loads[1].wait()
    start = jnp.broadcast_to(start_ref[...].astype(jnp.float32), (days, rows)).T
    day = lax.broadcasted_iota(jnp.int32, (rows, days), 1).astype(jnp.float32)
    y = jnp.where(day >= start, ret_ref[...].astype(jnp.float32), 0.0)
    sigma = sigma_of(y)
    sigma_ref[...] = jnp.broadcast_to(sigma, sigma_ref.shape)
    masked = y.astype(jnp.bfloat16)
    masked_ref[...] = masked
    both_ref[:, :days] = masked
    loads[2].wait()
    both_ref[:, days:] = (sigma * w_ref[...].astype(jnp.float32)).astype(jnp.bfloat16)


def sigma_of(y):
    sq = (y * y).astype(jnp.bfloat16).astype(jnp.float32)
    obs = jnp.where(y != 0.0, 1.0, 0.0)
    total = jnp.sum(sq, axis=1, keepdims=True)
    count = jnp.sum(obs, axis=1, keepdims=True)
    return jnp.sqrt(total / jnp.maximum(count, 1.0) + 1e-06)


def nt(a, b):
    return lax.dot_general(a, b, (((1,), (1,)), ((), ())), preferred_element_type=jnp.float32)


def parts_of(y):
    wide = y.astype(jnp.float32)
    obs = jnp.where(wide != 0.0, 1.0, 0.0).astype(jnp.bfloat16)
    return y, obs, (wide * wide).astype(jnp.bfloat16)


def chip_kernel(nrows, pairs, nin, has_diag, code_ref, *refs):
    ncols = sum(pairs)
    row_refs, col_refs = refs[:nrows], refs[nrows:nrows + ncols]
    in_refs, out_refs = refs[nrows + ncols:nrows + ncols + nin], refs[nrows + ncols + nin:]
    own, days = row_refs[0].shape
    delta = code_ref[0].astype(jnp.float32) / DENOM
    keep = 1.0 - delta
    ys, values, at = [], [], 0
    for n in pairs:
        if n == 1:
            ys.append(col_refs[at][:, :days])
            values.append(col_refs[at][:, days:])
        else:
            y = col_refs[at][...]
            ys.append(y)
            sigma = sigma_of(y.astype(jnp.float32))
            values.append((sigma * col_refs[at + 1][...].astype(jnp.float32)).astype(jnp.bfloat16))
        at += n
    cols = [parts_of(y) for y in ys]
    values = jnp.concatenate(values)
    for i, r in enumerate(row_refs):
        ry, ro, rs = parts_of(r[...])
        shrunk = []
        for j, (cy, co, cs) in enumerate(cols):
            cross, left, right = nt(ry, cy), nt(rs, co), nt(ro, cs)
            part = keep * (cross * lax.rsqrt(left * right + 1e-06))
            if has_diag and i == 0 and j == 0:
                a = lax.broadcasted_iota(jnp.int32, part.shape, 0)
                b = lax.broadcasted_iota(jnp.int32, part.shape, 1)
                part = part + jnp.where(a == b, delta, 0.0)
            shrunk.append(part.astype(jnp.bfloat16))
        term = jnp.dot(jnp.concatenate(shrunk, 1), values, preferred_element_type=jnp.float32)
        if nin:
            term = term + in_refs[i][...]
        out_refs[i][...] = term.astype(out_refs[i].dtype)


def final_kernel(sigma_ref, *refs):
    out_ref = refs[-1]
    total = refs[0][...]
    for r in refs[1:-1]:
        total = total + r[...].astype(jnp.float32)
    out_ref[...] = sigma_ref[:, :1] * total


def call(kernel, args, outs, specs=None, scratch=(), aliases=None):
    return pl.pallas_call(
        kernel,
        out_shape=outs,
        in_specs=specs or [vspec() for _ in args],
        out_specs=jax.tree.map(lambda _: vspec(), outs),
        scratch_shapes=scratch,
        input_output_aliases=aliases or {},
        compiler_params=pltpu.CompilerParams(vmem_limit_bytes=48 * 1024 * 1024),
    )(*args)


def after(value, *others):
    return lax.optimization_barrier((value, *others))[0]


def per_device(nrow, ncol, returns, start_day, shrink_code, weights):
    own, days = returns.shape
    ports = weights.shape[1]
    far_y, far_z = nrow // 2, ncol // 4
    ys, zs = range(1, far_y), range(1, far_z)

    def send(value, y=0, x=0, zh=0, zl=0, core=0):
        pairs = []
        for r in range(nrow):
            for c in range(ncol):
                rr = (r // 2 + y) % far_y * 2 + (r % 2 + x) % 2
                cc = (c // 4 + zh) % far_z * 4 + (c // 2 % 2 + zl) % 2 * 2 + (c % 2 + core) % 2
                pairs.append((r * ncol + c, rr * ncol + cc))
        return lax.ppermute(value, ("row", "col"), pairs)

    smem = pl.BlockSpec(memory_space=pltpu.SMEM)
    shape = jax.ShapeDtypeStruct
    masked, both, sigma = call(
        prep_kernel,
        tuple(
            pltpu.with_memory_space_constraint(v, pltpu.HBM)
            for v in (start_day.reshape(1, own), returns, weights)
        ),
        (
            shape((own, days), jnp.bfloat16),
            shape((own, days + ports), jnp.bfloat16),
            shape((own, 128), jnp.float32),
        ),
        [pl.BlockSpec(memory_space=pltpu.HBM)] * 3,
        [
            VMEM((1, own), jnp.int32),
            VMEM((own, days), jnp.bfloat16),
            VMEM((own, ports), jnp.bfloat16),
            pltpu.SemaphoreType.DMA((3,)),
        ],
    )
    total, rows = [], []

    def chip(*pieces, last=False):
        first = not total
        new = {}
        for part in ((3,), (1, 2, 0)) if last else (range(4),):
            into = [] if first else [total[i] for i in part]
            args = (shrink_code, *(rows[i] for i in part), *(a for p in pieces for a in p), *into)
            kinds = [jnp.bfloat16 if last and i else jnp.float32 for i in part]
            made = call(
                functools.partial(chip_kernel, len(part), tuple(map(len, pieces)), len(into), first),
                args,
                [VMEM((own, ports), kind) for kind in kinds],
                [smem] + [vspec() for _ in args[1:]],
                aliases=None if last else {len(args) - len(into) + k: k for k in range(len(into))},
            )
            new.update(zip(part, made))
        total[:] = [new[i] for i in range(4)]
        return list(total)

    at = {}
    at["zh_w"] = [send(weights, zh=k) for k in zs]
    at["zh_m"] = [send(masked, zh=k) for k in zs]
    at["near_w"] = [send(weights, y=k) for k in ys]
    at["near_m"] = [send(masked, y=k) for k in ys]
    at["x"] = [send(masked, x=1)]
    at["xzl"] = [send(at["x"][0], zl=1)]
    at["fwd_w"] = [send(v, y=k) for v in at["zh_w"] for k in ys]
    at["nm_s"] = [send(v, core=1) for v in at["near_m"]]
    at["m_s"] = [send(v, core=1) for v in at["zh_m"]]
    at["fwd_m"] = [send(after(v, *at["xzl"]), y=k) for v in at["zh_m"] for k in ys]
    at["w_s"] = [send(after(v, *at["zh_m"]), core=1) for v in at["zh_w"]]
    at["nw_s"] = [send(v, core=1) for v in at["near_w"]]
    at["zl"] = [send(masked, zl=1)]
    at["own_s"] = [send(after(both, *at["near_m"], *at["zl"]), core=1)]
    rows += [masked, at["x"][0], at["zl"][0], at["xzl"][0]]
    at["K1"] = chip((after(both, *at["zh_w"]),), (at["own_s"][0],), *zip((*at["near_m"], *at["nm_s"]), (*at["near_w"], *at["nw_s"])))
    at["K2"] = at["K1"]
    at["fw_s"] = [send(v, core=1) for v in at["fwd_w"]]
    for a, b, p, q in zip(at["zh_m"], at["zh_w"], at["m_s"], at["w_s"]):
        at["K3"] = chip((a, b), (p, q))
    at["fm_s"] = [send(after(v, *at["K2"]), core=1) for v in at["fwd_m"]]
    tail = list(zip(at["fwd_m"], at["fwd_w"], at["fm_s"], at["fw_s"]))
    for k, (a, b, p, q) in enumerate(tail):
        chip((a, b), (p, q), last=k == len(tail) - 1)

    arrived = [total[0]]
    for i, x, zl in ((3, 1, 1), (1, 1, 0), (2, 0, 1)):
        arrived.append(send(total[i], x=x, zl=zl))
    return call(final_kernel, (sigma, *arrived), shape((own, ports), jnp.float32))


def solution(mesh):
    in_specs = (P(("col", "row"), None), P(("col", "row")), P(), P(("col", "row"), None))
    out_specs = P(("col", "row"), None)
    body = functools.partial(per_device, mesh.shape["row"], mesh.shape["col"])
    return jax.shard_map(
        body, mesh=mesh, in_specs=in_specs, out_specs=out_specs, check_vma=False
    )
```

```python
import functools

import jax
import jax.numpy as jnp
from jax import lax
from jax.experimental import pallas as pl
from jax.experimental.pallas import tpu as pltpu
from jax.sharding import PartitionSpec as P

DENOM = 256
VMEM = pltpu.VMEM


def vspec():
    return pl.BlockSpec(memory_space=VMEM)


def prep_kernel(start_hbm, ret_hbm, w_hbm, *refs):
    masked_ref, both_ref, sigma_ref, start_ref, ret_ref, w_ref, sems = refs
    loads = [
        pltpu.make_async_copy(src, dst, sems.at[k])
        for k, (src, dst) in enumerate(((start_hbm, start_ref), (ret_hbm, ret_ref), (w_hbm, w_ref)))
    ]
    for load in loads:
        load.start()
    rows, days = ret_ref.shape
    loads[0].wait()
    loads[1].wait()
    start = jnp.broadcast_to(start_ref[...].astype(jnp.float32), (days, rows)).T
    day = lax.broadcasted_iota(jnp.int32, (rows, days), 1).astype(jnp.float32)
    y = jnp.where(day >= start, ret_ref[...].astype(jnp.float32), 0.0)
    sigma = sigma_of(y)
    sigma_ref[...] = jnp.broadcast_to(sigma, sigma_ref.shape)
    masked = y.astype(jnp.bfloat16)
    masked_ref[...] = masked
    both_ref[:, :days] = masked
    loads[2].wait()
    both_ref[:, days:] = (sigma * w_ref[...].astype(jnp.float32)).astype(jnp.bfloat16)


def sigma_of(y):
    sq = (y * y).astype(jnp.bfloat16).astype(jnp.float32)
    obs = jnp.where(y != 0.0, 1.0, 0.0)
    total = jnp.sum(sq, axis=1, keepdims=True)
    count = jnp.sum(obs, axis=1, keepdims=True)
    return jnp.sqrt(total / jnp.maximum(count, 1.0) + 1e-06)


def nt(a, b):
    return lax.dot_general(a, b, (((1,), (1,)), ((), ())), preferred_element_type=jnp.float32)


def parts_of(y):
    wide = y.astype(jnp.float32)
    obs = jnp.where(wide != 0.0, 1.0, 0.0).astype(jnp.bfloat16)
    return y, obs, (wide * wide).astype(jnp.bfloat16)


def chip_kernel(nrows, pairs, nin, has_diag, code_ref, *refs):
    ncols = sum(pairs)
    row_refs, col_refs = refs[:nrows], refs[nrows:nrows + ncols]
    in_refs, out_refs = refs[nrows + ncols:nrows + ncols + nin], refs[nrows + ncols + nin:]
    own, days = row_refs[0].shape
    delta = code_ref[0].astype(jnp.float32) / DENOM
    keep = 1.0 - delta
    ys, values, at = [], [], 0
    for n in pairs:
        if n == 1:
            ys.append(col_refs[at][:, :days])
            values.append(col_refs[at][:, days:])
        else:
            y = col_refs[at][...]
            ys.append(y)
            sigma = sigma_of(y.astype(jnp.float32))
            values.append((sigma * col_refs[at + 1][...].astype(jnp.float32)).astype(jnp.bfloat16))
        at += n
    cols = [parts_of(y) for y in ys]
    values = jnp.concatenate(values)
    for i, r in enumerate(row_refs):
        ry, ro, rs = parts_of(r[...])
        shrunk = []
        for j, (cy, co, cs) in enumerate(cols):
            cross, left, right = nt(ry, cy), nt(rs, co), nt(ro, cs)
            part = keep * (cross * lax.rsqrt(left * right + 1e-06))
            if has_diag and i == 0 and j == 0:
                a = lax.broadcasted_iota(jnp.int32, part.shape, 0)
                b = lax.broadcasted_iota(jnp.int32, part.shape, 1)
                part = part + jnp.where(a == b, delta, 0.0)
            shrunk.append(part.astype(jnp.bfloat16))
        term = jnp.dot(jnp.concatenate(shrunk, 1), values, preferred_element_type=jnp.float32)
        if nin:
            term = term + in_refs[i][...]
        out_refs[i][...] = term.astype(out_refs[i].dtype)


def final_kernel(sigma_ref, *refs):
    out_ref = refs[-1]
    total = refs[0][...]
    for r in refs[1:-1]:
        total = total + r[...].astype(jnp.float32)
    out_ref[...] = sigma_ref[:, :1] * total


def call(kernel, args, outs, specs=None, scratch=(), aliases=None):
    return pl.pallas_call(
        kernel,
        out_shape=outs,
        in_specs=specs or [vspec() for _ in args],
        out_specs=jax.tree.map(lambda _: vspec(), outs),
        scratch_shapes=scratch,
        input_output_aliases=aliases or {},
        compiler_params=pltpu.CompilerParams(vmem_limit_bytes=48 * 1024 * 1024),
    )(*args)


def after(value, *others):
    return lax.optimization_barrier((value, *others))[0]


def per_device(nrow, ncol, returns, start_day, shrink_code, weights):
    own, days = returns.shape
    ports = weights.shape[1]
    far_y, far_z = nrow // 2, ncol // 4
    ys, zs = range(1, far_y), range(1, far_z)

    def send(value, y=0, x=0, zh=0, zl=0, core=0):
        pairs = []
        for r in range(nrow):
            for c in range(ncol):
                rr = (r // 2 + y) % far_y * 2 + (r % 2 + x) % 2
                cc = (c // 4 + zh) % far_z * 4 + (c // 2 % 2 + zl) % 2 * 2 + (c % 2 + core) % 2
                pairs.append((r * ncol + c, rr * ncol + cc))
        return lax.ppermute(value, ("row", "col"), pairs)

    smem = pl.BlockSpec(memory_space=pltpu.SMEM)
    shape = jax.ShapeDtypeStruct
    masked, both, sigma = call(
        prep_kernel,
        tuple(
            pltpu.with_memory_space_constraint(v, pltpu.HBM)
            for v in (start_day.reshape(1, own), returns, weights)
        ),
        (
            shape((own, days), jnp.bfloat16),
            shape((own, days + ports), jnp.bfloat16),
            shape((own, 128), jnp.float32),
        ),
        [pl.BlockSpec(memory_space=pltpu.HBM)] * 3,
        [
            VMEM((1, own), jnp.int32),
            VMEM((own, days), jnp.bfloat16),
            VMEM((own, ports), jnp.bfloat16),
            pltpu.SemaphoreType.DMA((3,)),
        ],
    )
    total, rows = [], []

    def chip(*pieces, last=False):
        first = not total
        new = {}
        for part in ((3,), (1, 2, 0)) if last else (range(4),):
            into = [] if first else [total[i] for i in part]
            args = (shrink_code, *(rows[i] for i in part), *(a for p in pieces for a in p), *into)
            kinds = [jnp.bfloat16 if last and i else jnp.float32 for i in part]
            made = call(
                functools.partial(chip_kernel, len(part), tuple(map(len, pieces)), len(into), first),
                args,
                [VMEM((own, ports), kind) for kind in kinds],
                [smem] + [vspec() for _ in args[1:]],
                aliases=None if last else {len(args) - len(into) + k: k for k in range(len(into))},
            )
            new.update(zip(part, made))
        total[:] = [new[i] for i in range(4)]
        return list(total)

    at = {}
    at["zh_w"] = [send(weights, zh=k) for k in zs]
    at["zh_m"] = [send(masked, zh=k) for k in zs]
    at["near_w"] = [send(weights, y=k) for k in ys]
    at["x"] = [send(masked, x=1)]
    at["xzl"] = [send(at["x"][0], zl=1)]
    at["fwd_w"] = [send(v, y=k) for v in at["zh_w"] for k in ys]
    at["fw_s"] = [send(v, core=1) for v in at["fwd_w"]]
    at["m_s"] = [send(v, core=1) for v in at["zh_m"]]
    at["fwd_m"] = [send(after(v, *at["xzl"]), y=k) for v in at["zh_m"] for k in ys]
    at["w_s"] = [send(v, core=1) for v in at["zh_w"]]
    at["nw_s"] = [send(v, core=1) for v in at["near_w"]]
    at["zl"] = [send(masked, zl=1)]
    at["own_s"] = [send(after(both, *at["zl"]), core=1)]
    at["near_m"] = [send(masked, y=k) for k in ys]
    at["nm_s"] = [send(v, core=1) for v in at["near_m"]]
    rows += [masked, at["x"][0], at["zl"][0], at["xzl"][0]]
    at["K1"] = chip((after(both, *at["zh_w"], *at["near_w"]),), (at["own_s"][0],), *zip((*at["near_m"], *at["nm_s"]), (*at["near_w"], *at["nw_s"])))
    at["K2"] = at["K1"]
    for a, b, p, q in zip(at["zh_m"], at["zh_w"], at["m_s"], at["w_s"]):
        at["K3"] = chip((a, b), (p, q))
    at["fm_s"] = [send(after(v, *at["K2"]), core=1) for v in at["fwd_m"]]
    tail = list(zip(at["fwd_m"], at["fwd_w"], at["fm_s"], at["fw_s"]))
    for k, (a, b, p, q) in enumerate(tail):
        chip((a, b), (p, q), last=k == len(tail) - 1)

    arrived = [total[0]]
    for i, x, zl in ((3, 1, 1), (1, 1, 0), (2, 0, 1)):
        arrived.append(send(total[i], x=x, zl=zl))
    return call(final_kernel, (sigma, *arrived), shape((own, ports), jnp.float32))


def solution(mesh):
    in_specs = (P(("col", "row"), None), P(("col", "row")), P(), P(("col", "row"), None))
    out_specs = P(("col", "row"), None)
    body = functools.partial(per_device, mesh.shape["row"], mesh.shape["col"])
    return jax.shard_map(
        body, mesh=mesh, in_specs=in_specs, out_specs=out_specs, check_vma=False
    )
```

```python
import functools

import jax
import jax.numpy as jnp
from jax import lax
from jax.experimental import pallas as pl
from jax.experimental.pallas import tpu as pltpu
from jax.sharding import PartitionSpec as P

DENOM = 256
VMEM = pltpu.VMEM


def vspec():
    return pl.BlockSpec(memory_space=VMEM)


def prep_kernel(start_hbm, ret_hbm, w_hbm, *refs):
    masked_ref, both_ref, sigma_ref, start_ref, ret_ref, w_ref, sems = refs
    loads = [
        pltpu.make_async_copy(src, dst, sems.at[k])
        for k, (src, dst) in enumerate(((start_hbm, start_ref), (ret_hbm, ret_ref), (w_hbm, w_ref)))
    ]
    for load in loads:
        load.start()
    rows, days = ret_ref.shape
    loads[0].wait()
    loads[1].wait()
    start = jnp.broadcast_to(start_ref[...].astype(jnp.float32), (days, rows)).T
    day = lax.broadcasted_iota(jnp.int32, (rows, days), 1).astype(jnp.float32)
    y = jnp.where(day >= start, ret_ref[...].astype(jnp.float32), 0.0)
    sigma = sigma_of(y)
    sigma_ref[...] = jnp.broadcast_to(sigma, sigma_ref.shape)
    masked = y.astype(jnp.bfloat16)
    masked_ref[...] = masked
    both_ref[:, :days] = masked
    loads[2].wait()
    both_ref[:, days:] = (sigma * w_ref[...].astype(jnp.float32)).astype(jnp.bfloat16)


def sigma_of(y):
    sq = (y * y).astype(jnp.bfloat16).astype(jnp.float32)
    obs = jnp.where(y != 0.0, 1.0, 0.0)
    total = jnp.sum(sq, axis=1, keepdims=True)
    count = jnp.sum(obs, axis=1, keepdims=True)
    return jnp.sqrt(total / jnp.maximum(count, 1.0) + 1e-06)


def nt(a, b):
    return lax.dot_general(a, b, (((1,), (1,)), ((), ())), preferred_element_type=jnp.float32)


def parts_of(y):
    wide = y.astype(jnp.float32)
    obs = jnp.where(wide != 0.0, 1.0, 0.0).astype(jnp.bfloat16)
    return y, obs, (wide * wide).astype(jnp.bfloat16)


def chip_kernel(nrows, pairs, nin, has_diag, code_ref, *refs):
    ncols = sum(pairs)
    row_refs, col_refs = refs[:nrows], refs[nrows:nrows + ncols]
    in_refs, out_refs = refs[nrows + ncols:nrows + ncols + nin], refs[nrows + ncols + nin:]
    own, days = row_refs[0].shape
    delta = code_ref[0].astype(jnp.float32) / DENOM
    keep = 1.0 - delta
    ys, values, at = [], [], 0
    for n in pairs:
        if n == 1:
            ys.append(col_refs[at][:, :days])
            values.append(col_refs[at][:, days:])
        else:
            y = col_refs[at][...]
            ys.append(y)
            sigma = sigma_of(y.astype(jnp.float32))
            values.append((sigma * col_refs[at + 1][...].astype(jnp.float32)).astype(jnp.bfloat16))
        at += n
    cols = [parts_of(y) for y in ys]
    values = jnp.concatenate(values)
    for i, r in enumerate(row_refs):
        ry, ro, rs = parts_of(r[...])
        shrunk = []
        for j, (cy, co, cs) in enumerate(cols):
            cross, left, right = nt(ry, cy), nt(rs, co), nt(ro, cs)
            part = keep * (cross * lax.rsqrt(left * right + 1e-06))
            if has_diag and i == 0 and j == 0:
                a = lax.broadcasted_iota(jnp.int32, part.shape, 0)
                b = lax.broadcasted_iota(jnp.int32, part.shape, 1)
                part = part + jnp.where(a == b, delta, 0.0)
            shrunk.append(part.astype(jnp.bfloat16))
        term = jnp.dot(jnp.concatenate(shrunk, 1), values, preferred_element_type=jnp.float32)
        if nin:
            term = term + in_refs[i][...]
        out_refs[i][...] = term.astype(out_refs[i].dtype)


def final_kernel(sigma_ref, *refs):
    out_hbm, out_ref, sems = refs[-3:]
    rows = out_ref.shape[0]
    parts = sems.shape[0]
    step = rows // parts
    stores = []
    for k in range(parts):
        at = slice(k * step, (k + 1) * step)
        total = refs[0][at]
        for r in refs[1:-3]:
            total = total + r[at].astype(jnp.float32)
        out_ref[at] = sigma_ref[at, :1] * total
        stores.append(pltpu.make_async_copy(out_ref.at[at], out_hbm.at[at], sems.at[k]))
        stores[-1].start()
    for store in stores:
        store.wait()


def call(kernel, args, outs, specs=None, scratch=(), aliases=None, out_spec=None):
    return pl.pallas_call(
        kernel,
        out_shape=outs,
        in_specs=specs or [vspec() for _ in args],
        out_specs=out_spec or jax.tree.map(lambda _: vspec(), outs),
        scratch_shapes=scratch,
        input_output_aliases=aliases or {},
        compiler_params=pltpu.CompilerParams(vmem_limit_bytes=48 * 1024 * 1024),
    )(*args)


def after(value, *others):
    return lax.optimization_barrier((value, *others))[0]


def per_device(nrow, ncol, returns, start_day, shrink_code, weights):
    own, days = returns.shape
    ports = weights.shape[1]
    far_y, far_z = nrow // 2, ncol // 4
    ys, zs = range(1, far_y), range(1, far_z)

    def send(value, y=0, x=0, zh=0, zl=0, core=0):
        pairs = []
        for r in range(nrow):
            for c in range(ncol):
                rr = (r // 2 + y) % far_y * 2 + (r % 2 + x) % 2
                cc = (c // 4 + zh) % far_z * 4 + (c // 2 % 2 + zl) % 2 * 2 + (c % 2 + core) % 2
                pairs.append((r * ncol + c, rr * ncol + cc))
        return lax.ppermute(value, ("row", "col"), pairs)

    smem = pl.BlockSpec(memory_space=pltpu.SMEM)
    shape = jax.ShapeDtypeStruct
    masked, both, sigma = call(
        prep_kernel,
        tuple(
            pltpu.with_memory_space_constraint(v, pltpu.HBM)
            for v in (start_day.reshape(1, own), returns, weights)
        ),
        (
            shape((own, days), jnp.bfloat16),
            shape((own, days + ports), jnp.bfloat16),
            shape((own, 128), jnp.float32),
        ),
        [pl.BlockSpec(memory_space=pltpu.HBM)] * 3,
        [
            VMEM((1, own), jnp.int32),
            VMEM((own, days), jnp.bfloat16),
            VMEM((own, ports), jnp.bfloat16),
            pltpu.SemaphoreType.DMA((3,)),
        ],
    )
    total, rows = [], []

    def chip(*pieces, last=False):
        first = not total
        new = {}
        for part in ((3,), (1, 2, 0)) if last else (range(4),):
            into = [] if first else [total[i] for i in part]
            args = (shrink_code, *(rows[i] for i in part), *(a for p in pieces for a in p), *into)
            kinds = [jnp.bfloat16 if last and i else jnp.float32 for i in part]
            made = call(
                functools.partial(chip_kernel, len(part), tuple(map(len, pieces)), len(into), first),
                args,
                [VMEM((own, ports), kind) for kind in kinds],
                [smem] + [vspec() for _ in args[1:]],
                aliases=None if last else {len(args) - len(into) + k: k for k in range(len(into))},
            )
            new.update(zip(part, made))
        total[:] = [new[i] for i in range(4)]
        return list(total)

    at = {}
    at["zh_w"] = [send(weights, zh=k) for k in zs]
    at["zh_m"] = [send(masked, zh=k) for k in zs]
    at["near_w"] = [send(weights, y=k) for k in ys]
    at["x"] = [send(masked, x=1)]
    at["xzl"] = [send(at["x"][0], zl=1)]
    at["fwd_w"] = [send(v, y=k) for v in at["zh_w"] for k in ys]
    at["fw_s"] = [send(v, core=1) for v in at["fwd_w"]]
    at["m_s"] = [send(v, core=1) for v in at["zh_m"]]
    at["fwd_m"] = [send(after(v, *at["xzl"]), y=k) for v in at["zh_m"] for k in ys]
    at["w_s"] = [send(v, core=1) for v in at["zh_w"]]
    at["nw_s"] = [send(v, core=1) for v in at["near_w"]]
    at["zl"] = [send(masked, zl=1)]
    at["own_s"] = [send(after(both, *at["zl"]), core=1)]
    at["near_m"] = [send(masked, y=k) for k in ys]
    at["nm_s"] = [send(v, core=1) for v in at["near_m"]]
    rows += [masked, at["x"][0], at["zl"][0], at["xzl"][0]]
    at["K1"] = chip((after(both, *at["zh_w"], *at["near_w"]),), (at["own_s"][0],), *zip((*at["near_m"], *at["nm_s"]), (*at["near_w"], *at["nw_s"])))
    at["K2"] = at["K1"]
    for a, b, p, q in zip(at["zh_m"], at["zh_w"], at["m_s"], at["w_s"]):
        at["K3"] = chip((a, b), (p, q))
    at["fm_s"] = [send(after(v, *at["K2"]), core=1) for v in at["fwd_m"]]
    tail = list(zip(at["fwd_m"], at["fwd_w"], at["fm_s"], at["fw_s"]))
    for k, (a, b, p, q) in enumerate(tail):
        chip((a, b), (p, q), last=k == len(tail) - 1)

    arrived = [total[0]]
    for i, x, zl in ((3, 1, 1), (1, 1, 0), (2, 0, 1)):
        arrived.append(send(total[i], x=x, zl=zl))
    return call(
        final_kernel,
        (sigma, *arrived),
        shape((own, ports), jnp.float32),
        scratch=[VMEM((own, ports), jnp.float32), pltpu.SemaphoreType.DMA((4,))],
        out_spec=pl.BlockSpec(memory_space=pltpu.HBM),
    )


def solution(mesh):
    in_specs = (P(("col", "row"), None), P(("col", "row")), P(), P(("col", "row"), None))
    out_specs = P(("col", "row"), None)
    body = functools.partial(per_device, mesh.shape["row"], mesh.shape["col"])
    return jax.shard_map(
        body, mesh=mesh, in_specs=in_specs, out_specs=out_specs, check_vma=False
    )
```
